32 devices in a mesh: groups: 2 (over y), front: 4 (over z), batch: 2 (over x), line: 2 (over core).
Axes of the slice: x: 2, y: 2, z: 4, core: 2. Of those that a mesh axis runs over, the one named last changes fastest.
Arguments:
- injections: float32 [2048, 512], P('front', ('groups', 'batch')), parts along dimension 1, may hold values from -6 to 6
- switch_from: int32 [2, 512], P(None, ('groups', 'batch')), parts along dimension 1, may hold values from 0 to 2047
- switch_to: int32 [2, 512], P(None, ('groups', 'batch')), parts along dimension 1, may hold values from 0 to 2047
- switch_susc: float32 [2, 512], P(None, ('groups', 'batch')), parts along dimension 1, may hold values from 0.5 to 4
- coupling: float32 [2048, 512], P('front'), may hold values from -1 to 1
- pivot_inverse: float32 [2048, 512], P('front')
- branch_from: int32 [4096], P(('front', 'line')), may hold values from 0 to 2047, as said below
- branch_to: int32 [4096], P(('front', 'line')), may hold values from 0 to 2047, as said below
- branch_susc: float32 [4096], P(('front', 'line')), may hold values from 0.5 to 2
- branch_owner: int32 [4096, 1], P(('front', 'line')), may hold values from 0 to 7; in each aligned block of 512 rows (0 to 511, 512 to 1023, ...) at most 128 rows name the same one
- in_weight: float32 [128], replicated, may hold values from -4 to 4
- in_bias: float32 [128], replicated, may hold values from -1 to 1
- out_weight: bfloat16 [128, 128], replicated, may hold values from -0.5 to 0.5
Outputs:
- region_scores: bfloat16 [8, 512, 128], P(('front', 'line'), ('groups', 'batch')), parts along dimension 1
- angles: float32 [2048, 512], P('front', ('groups', 'batch')), parts along dimension 1
The draws below stay inside these ranges and needn't reach their ends.
There are 2 independent parts, one for each index of `groups`. The reference program is written for one: setup_inputs(seed, part) draws one part's arguments, and reference() takes and returns one part's arrays. A program takes and returns all parts, laid end to end along the dimension named above; an argument that names none is the same for every part. Nothing has to cross between parts.
Inputs may be any that keep to these rules, and one draw needn't show every extreme that they name: `branch_from`: the bus of row r lies in slab s = r // 1024, between s * 512 and s * 512 + 511. `branch_to`: the bus of row r lies in slab s = r // 1024 or in slab s + 1. `branch_owner`: in each aligned block of 512 rows (the branches of one device) no owner is named by more than 128 rows.
All inputs are finite; a program needn't handle non-finite values.
Results may differ from the reference program's by a relative error of at most 0.005.
Values sent between devices are 32-bit elements; how exact they have to be, the bound alone decides.
A program may use at most 64 MiB of HBM per device.

```python
import math
import jax
import jax.numpy as jnp
import numpy as np
from jax import lax

NB = 512
K = 2
H = 128
BR_DEV = 512
NBUS = 2048
TOPOS = 256
OWNERS = 8
CAP = 128
SLAB_BR = 1024
NBR = 4096
N_FRONT = 4


def draw_coupling(key, part):
    key_off = jax.random.fold_in(key, 21)
    key_mag = jax.random.fold_in(key, 22)
    key_sign = jax.random.fold_in(key, 23)
    off_noise = jax.random.uniform(key_off, (N_FRONT, NB, NB), jnp.float32, -1.0, 1.0) * (0.52 / NB ** 0.5)
    magnitude = jax.random.uniform(key_mag, (N_FRONT, NB), jnp.float32, 0.8, 0.95)
    sign_bits = jax.random.randint(key_sign, (N_FRONT, NB), 0, 2, dtype=jnp.int32)
    signs = (2 * sign_bits - 1).astype(jnp.float32)
    unit_diag = jnp.eye(NB, dtype=jnp.float32)
    blocks = off_noise * (1.0 - unit_diag) + (magnitude * signs)[:, :, None] * unit_diag
    return blocks.reshape(N_FRONT * NB, NB)


def draw_pivot_inverse(key, part):
    key_off = jax.random.fold_in(key, 3)
    key_diag = jax.random.fold_in(key, 5)
    uniform_noise = jax.random.uniform(key_off, (N_FRONT, NB, NB), jnp.float32, -1.0, 1.0)
    symmetric = (uniform_noise + jnp.transpose(uniform_noise, (0, 2, 1))) * (0.225 / NB)
    diagonal = jax.random.uniform(key_diag, (N_FRONT, NB), jnp.float32, 0.5, 0.8)
    unit_diag = jnp.eye(NB, dtype=jnp.float32)
    blocks = symmetric * (1.0 - unit_diag) + diagonal[:, :, None] * unit_diag
    return blocks.reshape(N_FRONT * NB, NB)


def branch_pair(key):
    pair_key = jax.random.fold_in(key, 11)
    key_from = jax.random.fold_in(pair_key, 1)
    key_to = jax.random.fold_in(pair_key, 2)
    key_tie = jax.random.fold_in(pair_key, 3)
    row_ids = jnp.arange(NBR, dtype=jnp.int32)
    slab_ids = row_ids // SLAB_BR
    from_bus = slab_ids * NB + jax.random.randint(key_from, (NBR,), 0, NB, dtype=jnp.int32)
    tie_flag = (jax.random.randint(key_tie, (NBR,), 0, 4, dtype=jnp.int32) == 0) & (slab_ids < N_FRONT - 1)
    to_bus = (slab_ids + tie_flag.astype(jnp.int32)) * NB + jax.random.randint(key_to, (NBR,), 0, NB, dtype=jnp.int32)
    return (from_bus, to_bus)


def draw_branch_from(key, part):
    return branch_pair(key)[0]


def draw_branch_to(key, part):
    return branch_pair(key)[1]


def set_ends(drawn, stream_key, smallest, top_value):
    longest = drawn.shape.index(max(drawn.shape))
    spots = []
    for shift in (0, 1):
        where = [jax.random.randint(jax.random.fold_in(stream_key, axis), (), 0, length) for axis, length in enumerate(drawn.shape)]
        where[longest] = (where[longest] + shift) % drawn.shape[longest]
        spots.append(tuple(where))
    return drawn.at[spots[0]].set(smallest).at[spots[1]].set(top_value)


def block_scale(key, dims, split, low, largest):
    level, own = 1.0, jax.random.fold_in(key, 6)
    for axis_at, parts in split:
        draws = jnp.exp(jax.random.uniform(jax.random.fold_in(own, axis_at), (parts,), jnp.float32, low / len(split), largest / len(split)))
        level = level * jnp.repeat(draws, dims[axis_at] // parts).reshape([-1 if axis == axis_at else 1 for axis in range(len(dims))])
    return level


def routed_block(stream_key, own, number, rows, number_of, top, most, slope):
    sequence = jax.random.permutation(stream_key, number_of)
    heavy_load, ordinary = shares(number_of, rows * top, most, slope, True), shares(number_of, rows * top, most, slope, False)
    places = jnp.arange(number_of)

    def named(tallies, rotation):
        used = int((tallies > 0).sum())
        fixed = max(1, used // 4)
        moved = fixed + (places - fixed + rotation * (used - fixed)) % max(1, number_of - fixed)
        return jnp.zeros((number_of,), jnp.int32).at[sequence[jnp.where(places < fixed, places, moved)]].set(jnp.asarray(tallies, jnp.int32))

    tallies = jnp.where(number % 4 == 0, named(heavy_load, number // 4), named(ordinary, number - number // 4 - 1))
    mixed = jax.random.permutation(jax.random.fold_in(own, 3), number_of)
    source_of, receiver = mixed[0:number_of // 2 * 2:2], mixed[1:number_of // 2 * 2:2]
    room = jnp.minimum(tallies[source_of] - 1, most - tallies[receiver]) // 2
    room = jnp.where((source_of == sequence[0]) | (receiver == sequence[0]) | (tallies[receiver] == 0), 0, jnp.maximum(room, 0))
    moved = jax.random.randint(jax.random.fold_in(own, 4), (number_of // 2,), 0, 1 << 20) % (room + 1)
    tallies = tallies.at[source_of].add(-moved).at[receiver].add(moved)
    members = jnp.searchsorted(jnp.cumsum(tallies), jnp.arange(rows * top), side="right").astype(jnp.int32)
    listing = members.reshape(top, rows).T
    listing = listing[jax.random.permutation(jax.random.fold_in(own, 1), rows)]
    rotation = jax.random.randint(jax.random.fold_in(own, 2), (rows, 1), 0, top)
    return jnp.take_along_axis(listing, (jnp.arange(top)[None, :] + rotation) % top, axis=1)


def shares(count, total, most, lean, full):
    loads = [(1 << 20) // math.isqrt(standing ** lean) + 1 for standing in range(1, count + 1)]
    largest = most if full else min(most, max(-(-total // count), total * loads[0] // sum(loads)))
    least = 1 if total - largest >= count - 1 else 0
    counts, spare = [largest] + [least] * (count - 1), total - largest - least * (count - 1)
    while spare > 0:
        candidates = [i for i in range(1, count) if counts[i] < largest] or [i for i in range(1, count) if counts[i] < most]
        mass, left = sum([loads[i] for i in candidates]), spare
        for i in candidates:
            extra = min(most - counts[i], max(1, left * loads[i] // mass), spare)
            counts[i] = counts[i] + extra
            spare = spare - extra
    return np.array(counts)


def scatter_about(rng, shape, spread, most, pieces=(), kind=jnp.bfloat16):
    values = jax.random.normal(rng, shape, jnp.float32) * spread
    if len(pieces) > 0:
        values = block_scale(rng, shape, pieces, -0.22, 0.18) * values
    return jnp.clip(values, min=-most, max=most).astype(kind)


def setup_inputs(seed: int = 0, part: int = 0) -> dict:
    seeds = jax.random.split(jax.random.key(seed), 14)
    own_keys = jax.random.split(jax.random.fold_in(seeds[13], part), 14)
    injections = scatter_about(own_keys[0], (NBUS, TOPOS), 1.0, 6.0, ((0, 4), (1, 2)), jnp.float32)
    switch_from = set_ends(jax.random.randint(own_keys[1], (K, TOPOS), 0, NBUS), jax.random.fold_in(own_keys[1], 1), 0, NBUS - 1).astype(jnp.int32)
    switch_to = set_ends(jax.random.randint(own_keys[2], (K, TOPOS), 0, NBUS), jax.random.fold_in(own_keys[2], 1), 0, NBUS - 1).astype(jnp.int32)
    switch_susc = jnp.clip(jnp.exp(math.log(4.0) - 2.0794415 * jax.random.uniform(own_keys[3], (K, TOPOS), jnp.float32) ** block_scale(own_keys[3], (K, TOPOS), ((1, 2),), -0.2, 0.2)), 0.5, 4.0)
    coupling = draw_coupling(jax.random.fold_in(seeds[13], 71), part)
    pivot_inverse = draw_pivot_inverse(jax.random.fold_in(seeds[13], 71), part)
    branch_from = draw_branch_from(jax.random.fold_in(seeds[13], 71), part)
    branch_to = draw_branch_to(jax.random.fold_in(seeds[13], 71), part)
    branch_susc = jnp.clip(jnp.exp(math.log(2.0) - 1.3862944 * jax.random.uniform(seeds[8], (NBR,), jnp.float32) ** block_scale(seeds[8], (NBR,), ((0, 8),), -0.2, 0.2)), 0.5, 2.0)
    branch_owner_keys = jax.random.split(jax.random.fold_in(seeds[9], 1), NBR // BR_DEV)
    branch_owner_turns = jax.random.permutation(jax.random.fold_in(seeds[9], 3), NBR // BR_DEV)
    branch_owner = jax.vmap(lambda own, number: routed_block(jax.random.fold_in(seeds[9], 2), own, number, BR_DEV, OWNERS, 1, CAP, 1))(branch_owner_keys, branch_owner_turns).reshape((NBR, 1))
    in_weight = scatter_about(seeds[10], (H,), 1.0, 4.0, (), jnp.float32)
    in_bias = jnp.clip(jax.random.uniform(seeds[11], (H,), jnp.float32, -1.0, 1.0), -1.0, 1.0)
    out_weight = scatter_about(seeds[12], (H, H), H ** -0.5, 0.5)
    return dict(injections=injections, switch_from=switch_from, switch_to=switch_to, switch_susc=switch_susc, coupling=coupling, pivot_inverse=pivot_inverse, branch_from=branch_from, branch_to=branch_to, branch_susc=branch_susc, branch_owner=branch_owner, in_weight=in_weight, in_bias=in_bias, out_weight=out_weight)


def product(operand, against):
    return jnp.dot(operand, against, precision=lax.Precision.HIGHEST, preferred_element_type=jnp.float32)

def centered_tanh(loadings, in_weight, in_bias):
    return jnp.tanh(loadings[..., None] * in_weight + in_bias) - jnp.tanh(in_bias)

def capacitance_solve(terms, switch_susc):
    switches = switch_susc.shape[0]
    factor = [[None] * switches for row_at in range(switches)]
    for row_at in range(switches):
        for col_at in range(row_at + 1):
            partial_sum = terms[row_at, 1 + col_at]
            if row_at == col_at:
                partial_sum = partial_sum + 1.0 / switch_susc[row_at]
            for inner_at in range(col_at):
                partial_sum = partial_sum - factor[row_at][inner_at] * factor[col_at][inner_at]
            if row_at == col_at:
                factor[row_at][col_at] = jnp.sqrt(partial_sum)
            else:
                factor[row_at][col_at] = partial_sum / factor[col_at][col_at]
    lower_part = []
    for row_at in range(switches):
        running = terms[row_at, 0]
        for inner_at in range(row_at):
            running = running - factor[row_at][inner_at] * lower_part[inner_at]
        lower_part.append(running / factor[row_at][row_at])
    weights = [None] * switches
    for row_at in reversed(range(switches)):
        running = lower_part[row_at]
        for inner_at in range(row_at + 1, switches):
            running = running - factor[inner_at][row_at] * weights[inner_at]
        weights[row_at] = running / factor[row_at][row_at]
    return jnp.stack(weights)

def reference(injections, switch_from, switch_to, switch_susc, coupling, pivot_inverse, branch_from, branch_to, branch_susc, branch_owner, in_weight, in_bias, out_weight):
    bus_ids = jnp.arange(NBUS, dtype=jnp.int32)
    from_hot = (bus_ids[:, None, None] == switch_from[None]).astype(jnp.float32)
    to_hot = (bus_ids[:, None, None] == switch_to[None]).astype(jnp.float32)
    incidence = from_hot - to_hot
    stacked = jnp.concatenate([injections[:, None, :], incidence], axis=1).reshape(N_FRONT, NB, (K + 1) * TOPOS)
    blocks_e = coupling.reshape(N_FRONT, NB, NB)
    blocks_p = pivot_inverse.reshape(N_FRONT, NB, NB)
    previous = jnp.zeros((NB, (K + 1) * TOPOS), jnp.float32)
    pivoted = []
    for slab_at in range(N_FRONT):
        current = stacked[slab_at] - product(blocks_e[slab_at], previous)
        pivoted.append(product(blocks_p[slab_at], current))
        previous = current
    upper_part = [None] * N_FRONT
    carried = jnp.zeros((NB, (K + 1) * TOPOS), jnp.float32)
    for slab_at in reversed(range(N_FRONT)):
        upper_part[slab_at] = pivoted[slab_at] - carried
        carried = product(blocks_e[slab_at].T, upper_part[slab_at])
    solved = jnp.concatenate(upper_part, axis=0).reshape(NBUS, K + 1, TOPOS)
    terms = jnp.einsum('bit,bct->ict', incidence, solved, precision=lax.Precision.HIGHEST)
    weights = capacitance_solve(terms, switch_susc)
    angles = solved[:, 0, :] - jnp.einsum('bit,it->bt', solved[:, 1:, :], weights, precision=lax.Precision.HIGHEST)
    flows = branch_susc[:, None] * (angles[branch_from] - angles[branch_to])
    owner_ids = branch_owner[:, 0]

    def pool_block(running, block_at):
        loadings = lax.dynamic_slice_in_dim(flows, block_at * BR_DEV, BR_DEV, 0)
        owner_part = lax.dynamic_slice_in_dim(owner_ids, block_at * BR_DEV, BR_DEV, 0)
        contrib = centered_tanh(loadings, in_weight, in_bias)
        return (running + jax.ops.segment_sum(contrib, owner_part, num_segments=OWNERS), None)
    start_sum = jnp.zeros((OWNERS, TOPOS, H), jnp.float32)
    summed, unused = lax.scan(pool_block, start_sum, jnp.arange(NBR // BR_DEV, dtype=jnp.int32))
    pooled = (summed * BR_DEV ** (-0.5)).astype(jnp.bfloat16)
    region_scores = jnp.dot(pooled.reshape(OWNERS * TOPOS, H), out_weight, preferred_element_type=jnp.float32)
    region_scores = region_scores.reshape(OWNERS, TOPOS, H).astype(jnp.bfloat16)
    return (region_scores, angles)
```

```python
import functools

import jax
import jax.numpy as jnp
from jax import lax
from jax.experimental import pallas as pl
from jax.experimental.pallas import tpu as pltpu
from jax.sharding import PartitionSpec as P

CHUNKS = 4
UNROLL = 8
SCALE = 512 ** (-0.5)
F32, BF16 = jnp.float32, jnp.bfloat16
VMEM_BYTES = 40 * 1024 * 1024


def split(value):
    high = value.astype(BF16)
    return high, (value - high.astype(F32)).astype(BF16)


def dot(operand, against):
    return jnp.dot(operand, against, preferred_element_type=F32)


def product(operand, against):
    high, low = split(operand)
    return dot(high, against[0]) + (dot(low, against[0]) + dot(high, against[1]))


def copy_to(src, dst, send_sem, recv_sem, front, line):
    return pltpu.make_async_remote_copy(
        src_ref=src,
        dst_ref=dst,
        send_sem=send_sem,
        recv_sem=recv_sem,
        device_id={"front": front, "line": line},
        device_id_type=pl.DeviceIdType.MESH,
    )


def greet(front, line):
    pl.semaphore_signal(
        pltpu.get_barrier_semaphore(),
        inc=1,
        device_id={"front": front, "line": line},
        device_id_type=pl.DeviceIdType.MESH,
    )


def capacitance_solve(terms, switch_susc):
    switches = len(switch_susc)
    factor = [[None] * switches for row_at in range(switches)]
    for row_at in range(switches):
        for col_at in range(row_at + 1):
            partial_sum = terms[row_at][1 + col_at]
            if row_at == col_at:
                partial_sum = partial_sum + 1.0 / switch_susc[row_at]
            for inner_at in range(col_at):
                partial_sum = partial_sum - factor[row_at][inner_at] * factor[col_at][inner_at]
            if row_at == col_at:
                factor[row_at][col_at] = jnp.sqrt(partial_sum)
            else:
                factor[row_at][col_at] = partial_sum / factor[col_at][col_at]
    lower_part = []
    for row_at in range(switches):
        running = terms[row_at][0]
        for inner_at in range(row_at):
            running = running - factor[row_at][inner_at] * lower_part[inner_at]
        lower_part.append(running / factor[row_at][row_at])
    weights = [None] * switches
    for row_at in reversed(range(switches)):
        running = lower_part[row_at]
        for inner_at in range(row_at + 1, switches):
            running = running - factor[inner_at][row_at] * weights[inner_at]
        weights[row_at] = running / factor[row_at][row_at]
    return weights


def solve_kernel(
    fronts, inj, sw_from, sw_to, sw_susc, coupling, pivot, joined,
    yown, yrecv, zown, town, trecv, wown, wrecv, cown, crecv, xfull, xnext, injt,
    e_fwd, e_back, p_fwd,
    y_s, y_r, t_s, t_r, w_s, w_r, c_s, c_r, x_s, x_r, n_s, n_r,
):
    me, line = lax.axis_index("front"), lax.axis_index("line")
    other = 1 - line
    first, last = me == 0, me == fronts - 1
    bus, topo = inj.shape
    switches = sw_from.shape[1]
    rows = topo // (2 * CHUNKS)
    kinds = switches + 1
    pairs = [(i, c) for i in range(switches) for c in range(i + 2)]

    greet(me, other)

    @pl.when(jnp.logical_not(first))
    def _():
        greet(me - 1, 0)
        greet(me - 1, 1)

    @pl.when(jnp.logical_not(last))
    def _():
        greet(me + 1, 0)
        greet(me + 1, 1)

    injt[...] = inj[...].T.reshape(injt.shape)

    def stack(c, carry):
        yown[c, 0:rows] = injt[line, c]
        ids = me * bus + lax.broadcasted_iota(jnp.int32, (rows, bus), 1)
        at = pl.ds(pl.multiple_of((line * CHUNKS + c) * rows, rows), rows)
        f, t = sw_from[at, :], sw_to[at, :]
        for i in range(switches):
            yown[c, (1 + i) * rows:(2 + i) * rows] = (ids == f[:, i:i + 1]).astype(F32) - (
                ids == t[:, i:i + 1]
            ).astype(F32)
        return carry

    lax.fori_loop(0, CHUNKS, stack, 0)
    pl.semaphore_wait(
        pltpu.get_barrier_semaphore(),
        1 + 2 * jnp.where(first, 0, 1) + 2 * jnp.where(last, 0, 1),
    )

    def y_copy(c):
        return copy_to(yown.at[c], yrecv.at[c], y_s.at[c], y_r.at[c], me + 1, line)

    def t_copy(c):
        return copy_to(town.at[c], trecv.at[c], t_s.at[c], t_r.at[c], me + 1, line)

    def w_copy(c):
        return copy_to(wown.at[c], wrecv.at[c], w_s.at[c], w_r.at[c], me - 1, line)

    def c_copy(c):
        return copy_to(cown.at[c], crecv.at[c], c_s.at[c], c_r.at[c], me - 1, line)

    def x_copy(c, half):
        place = xfull.at[half, c]
        return copy_to(place, place, x_s.at[c], x_r.at[c], me, other)

    def n_copy(c, half, to):
        return copy_to(
            xfull.at[half, c], xnext.at[half, c], n_s.at[to, c], n_r.at[half, c], me - 1, to
        )

    def each(fn):
        def step(c, carry):
            fn(c)
            return carry

        lax.fori_loop(0, CHUNKS, step, 0)

    @pl.when(first)
    def _():
        each(lambda c: y_copy(c).start())

    e_fwd[0], e_fwd[1] = split(coupling[...].T)
    p_fwd[0], p_fwd[1] = split(pivot[...].T)
    e_back[0], e_back[1] = split(coupling[...])
    lanes = lax.broadcasted_iota(jnp.int32, (rows, 128), 1)

    def back(c):
        w = wown[c]
        x = zown[c, 0:rows]
        for i in range(switches):
            x = x - zown[c, (1 + i) * rows:(2 + i) * rows] * w[:, i:i + 1]
        xfull[line, c] = x

        @pl.when(jnp.logical_not(last))
        def _():
            c_copy(c).wait_recv()
            xfull[line, c] = xfull[line, c] - crecv[c]

        @pl.when(jnp.logical_not(first))
        def _():
            cown[c] = product(xfull[line, c], e_back)
            c_copy(c).start()
            n_copy(c, line, 0).start()
            n_copy(c, line, 1).start()

        x_copy(c, line).start()

    def ahead(c):
        @pl.when(jnp.logical_not(first))
        def _():
            y_copy(c).wait_recv()
            yown[c] = yown[c] - product(yrecv[c], e_fwd)

            @pl.when(jnp.logical_not(last))
            def _():
                y_copy(c).start()

        y = yown[c]
        z = product(y, p_fwd)
        zown[c] = z
        block = jnp.zeros((rows, 128), F32)
        for j, (i, k) in enumerate(pairs):
            term = jnp.sum(
                y[(1 + i) * rows:(2 + i) * rows] * z[k * rows:(k + 1) * rows],
                axis=1, keepdims=True,
            )
            block = jnp.where(lanes == j, term, block)
        town[c] = block

        @pl.when(jnp.logical_not(first))
        def _():
            t_copy(c).wait_recv()
            town[c] = town[c] + trecv[c]

        @pl.when(jnp.logical_not(last))
        def _():
            t_copy(c).start()

        @pl.when(last)
        def _():
            total = town[c]
            terms = [[None] * kinds for i in range(switches)]
            for j, (i, k) in enumerate(pairs):
                terms[i][k] = total[:, j:j + 1]
            at = pl.ds(pl.multiple_of((line * CHUNKS + c) * rows, rows), rows)
            susc = sw_susc[at, :]
            weights = capacitance_solve(terms, [susc[:, i:i + 1] for i in range(switches)])
            w = jnp.zeros((rows, 128), F32)
            for i in range(switches):
                w = jnp.where(lanes == i, weights[i], w)
            wown[c] = w

            @pl.when(jnp.logical_not(first))
            def _():
                w_copy(c).start()

            back(c)

    each(ahead)

    @pl.when(jnp.logical_not(last))
    def _():
        def later(c):
            w_copy(c).wait_recv()
            wown[c] = wrecv[c]

            @pl.when(jnp.logical_not(first))
            def _():
                w_copy(c).start()

            back(c)

        each(later)

    each(lambda c: x_copy(c, other).wait_recv())
    joined[0:bus] = xfull[...].reshape(topo, bus).T

    @pl.when(last)
    def _():
        joined[bus:2 * bus] = jnp.zeros((bus, topo), F32)

    @pl.when(jnp.logical_not(last))
    def _():
        def arrive(c):
            n_copy(c, 0, 0).wait_recv()
            n_copy(c, 1, 0).wait_recv()

        each(arrive)
        joined[bus:2 * bus] = xnext[...].reshape(topo, bus).T

        def sent(c):
            y_copy(c).wait_send()
            t_copy(c).wait_send()

        each(sent)

    @pl.when(jnp.logical_not(first))
    def _():
        def sent(c):
            w_copy(c).wait_send()
            c_copy(c).wait_send()
            n_copy(c, line, 0).wait_send()
            n_copy(c, line, 1).wait_send()

        each(sent)

    each(lambda c: x_copy(c, line).wait_send())


def pool_kernel(br_from, br_to, br_susc, br_owner, joined, weight, bias, acc, wide_w, wide_b, wide_t):
    hidden, topo = wide_w.shape
    wide_w[...] = jnp.broadcast_to(weight[...], (hidden, topo))
    wide_b[...] = jnp.broadcast_to(bias[...], (hidden, topo))
    wide_t[...] = jnp.tanh(wide_b[...])
    acc[...] = jnp.zeros_like(acc)
    step_rows = 32

    def group(g, carry):
        flows, owners = [], []
        for u in range(UNROLL):
            at = g * UNROLL + u
            difference = joined[pl.ds(br_from[at], 1), :] - joined[pl.ds(br_to[at], 1), :]
            flows.append(br_susc[at] * difference)
            owners.append(br_owner[at])
        for h in range(0, hidden, step_rows):
            part = pl.ds(h, step_rows)
            w, b, t = wide_w[part, :], wide_b[part, :], wide_t[part, :]
            values = [jnp.tanh(flow * w + b) - t for flow in flows]
            for owner, value in zip(owners, values):
                acc[owner, part, :] += value
        return carry

    lax.fori_loop(0, br_from.shape[0] // UNROLL, group, 0)


def share_kernel(fronts, acc, out_weight, scores, paired, summed, arrived, p_s, p_r, s_s, s_r):
    me, line = lax.axis_index("front"), lax.axis_index("line")
    other = 1 - line
    greet(me, other)

    def hello(step, carry):
        greet(lax.rem(me + step, fronts), line)
        return carry

    lax.fori_loop(1, fronts, hello, 0)
    pl.semaphore_wait(pltpu.get_barrier_semaphore(), fronts)

    def p_copy(f):
        return copy_to(acc.at[f * 2 + other], paired.at[f], p_s.at[f], p_r.at[f], me, other)

    def s_copy(f, origin, slot):
        return copy_to(summed.at[f], arrived.at[origin], s_s.at[f], s_r.at[slot], f, line)

    def turn(fn, own):
        def step(at, carry):
            fn(lax.rem(me + at, fronts))
            return carry

        lax.fori_loop(1, fronts + own, step, 0)

    turn(lambda f: p_copy(f).start(), 1)

    def pair(f):
        p_copy(f).wait_recv()
        summed[f] = acc[f * 2 + line] + paired[f]

        @pl.when(f != me)
        def _():
            s_copy(f, me, me).start()

    turn(pair, 1)
    turn(lambda f: s_copy(f, f, f).wait_recv(), 0)
    arrived[me] = summed[me]

    def add(f, total):
        return total + arrived[f]

    total = lax.fori_loop(1, fronts, add, arrived[0])
    pooled = (total * SCALE).T.astype(BF16)
    scores[...] = dot(pooled, out_weight[...]).astype(BF16)
    turn(lambda f: p_copy(f).wait_send(), 1)
    turn(lambda f: s_copy(f, me, me).wait_send(), 0)


def body(
    injections, switch_from, switch_to, switch_susc, coupling, pivot_inverse,
    branch_from, branch_to, branch_susc, branch_owner, in_weight, in_bias, out_weight,
):
    fronts = lax.axis_size("front")
    bus, topo = injections.shape
    switches = switch_from.shape[0]
    hidden = in_weight.shape[0]
    rows = topo // (2 * CHUNKS)
    many = (switches + 1) * rows
    owners = lax.axis_size(("front", "line"))
    vmem = pl.BlockSpec(memory_space=pltpu.VMEM)
    smem = pl.BlockSpec(memory_space=pltpu.SMEM)
    dma = pltpu.SemaphoreType.DMA
    full = lambda *shape: pltpu.VMEM(shape, F32)
    half = pltpu.VMEM((2, bus, bus), BF16)

    joined = pl.pallas_call(
        functools.partial(solve_kernel, fronts),
        out_shape=jax.ShapeDtypeStruct((2 * bus, topo), F32),
        in_specs=[vmem] * 6,
        out_specs=vmem,
        scratch_shapes=[
            full(CHUNKS, many, bus), full(CHUNKS, many, bus), full(CHUNKS, many, bus),
            full(CHUNKS, rows, 128), full(CHUNKS, rows, 128),
            full(CHUNKS, rows, 128), full(CHUNKS, rows, 128),
            full(CHUNKS, rows, bus), full(CHUNKS, rows, bus),
            full(2, CHUNKS, rows, bus), full(2, CHUNKS, rows, bus), full(2, CHUNKS, rows, bus),
            half, half, half,
        ] + [dma((CHUNKS,))] * 10 + [dma((2, CHUNKS))] * 2,
        compiler_params=pltpu.CompilerParams(
            collective_id=0, has_side_effects=True, vmem_limit_bytes=VMEM_BYTES
        ),
        name="solve",
    )(injections, switch_from.T, switch_to.T, switch_susc.T, coupling, pivot_inverse)

    first_bus = lax.axis_index("front") * bus
    acc = pl.pallas_call(
        pool_kernel,
        out_shape=jax.ShapeDtypeStruct((owners, hidden, topo), F32),
        in_specs=[smem] * 4 + [vmem] * 3,
        out_specs=vmem,
        scratch_shapes=[full(hidden, topo)] * 3,
        compiler_params=pltpu.CompilerParams(vmem_limit_bytes=VMEM_BYTES),
        name="pool",
    )(
        jnp.clip(branch_from - first_bus, 0, 2 * bus - 1),
        jnp.clip(branch_to - first_bus, 0, 2 * bus - 1),
        branch_susc,
        jnp.clip(branch_owner[:, 0], 0, owners - 1),
        joined,
        in_weight[:, None],
        in_bias[:, None],
    )

    scores = pl.pallas_call(
        functools.partial(share_kernel, fronts),
        out_shape=jax.ShapeDtypeStruct((topo, out_weight.shape[1]), BF16),
        in_specs=[vmem] * 2,
        out_specs=vmem,
        scratch_shapes=[full(fronts, hidden, topo)] * 3 + [dma((fronts,))] * 4,
        compiler_params=pltpu.CompilerParams(
            collective_id=1, has_side_effects=True, vmem_limit_bytes=VMEM_BYTES
        ),
        name="share",
    )(acc, out_weight)
    return (scores[None], joined[0:bus])


def solution(mesh):
    in_specs = (
        P("front", ("groups", "batch")),
        P(None, ("groups", "batch")),
        P(None, ("groups", "batch")),
        P(None, ("groups", "batch")),
        P("front", None),
        P("front", None),
        P(("front", "line")),
        P(("front", "line")),
        P(("front", "line")),
        P(("front", "line"), None),
        P(),
        P(),
        P(),
    )
    out_specs = (P(("front", "line"), ("groups", "batch"), None), P("front", ("groups", "batch")))
    return jax.shard_map(body, mesh=mesh, in_specs=in_specs, out_specs=out_specs, check_vma=False)
```

```python
import functools

import jax
import jax.numpy as jnp
from jax import lax
from jax.experimental import pallas as pl
from jax.experimental.pallas import tpu as pltpu
from jax.sharding import PartitionSpec as P

CHUNKS = 4
UNROLL = 8
WIDE = 16
SCALE = 512 ** (-0.5)
F32, BF16 = jnp.float32, jnp.bfloat16
VMEM_BYTES = 40 * 1024 * 1024


def split(value):
    high = value.astype(BF16)
    return high, (value - high.astype(F32)).astype(BF16)


def dot(operand, against):
    return jnp.dot(operand, against, preferred_element_type=F32)


def product(operand, against):
    high, low = split(operand)
    rows = operand.shape[0]
    both = dot(jnp.concatenate([high, low], axis=0), against[0])
    return both[:rows] + (both[rows:] + dot(high, against[1]))


def copy_to(src, dst, send_sem, recv_sem, front, line):
    return pltpu.make_async_remote_copy(
        src_ref=src,
        dst_ref=dst,
        send_sem=send_sem,
        recv_sem=recv_sem,
        device_id={"front": front, "line": line},
        device_id_type=pl.DeviceIdType.MESH,
    )


def greet(front, line):
    pl.semaphore_signal(
        pltpu.get_barrier_semaphore(),
        inc=1,
        device_id={"front": front, "line": line},
        device_id_type=pl.DeviceIdType.MESH,
    )


def capacitance_solve(terms, switch_susc):
    switches = len(switch_susc)
    factor = [[None] * switches for row_at in range(switches)]
    for row_at in range(switches):
        for col_at in range(row_at + 1):
            partial_sum = terms[row_at][1 + col_at]
            if row_at == col_at:
                partial_sum = partial_sum + 1.0 / switch_susc[row_at]
            for inner_at in range(col_at):
                partial_sum = partial_sum - factor[row_at][inner_at] * factor[col_at][inner_at]
            if row_at == col_at:
                factor[row_at][col_at] = jnp.sqrt(partial_sum)
            else:
                factor[row_at][col_at] = partial_sum / factor[col_at][col_at]
    lower_part = []
    for row_at in range(switches):
        running = terms[row_at][0]
        for inner_at in range(row_at):
            running = running - factor[row_at][inner_at] * lower_part[inner_at]
        lower_part.append(running / factor[row_at][row_at])
    weights = [None] * switches
    for row_at in reversed(range(switches)):
        running = lower_part[row_at]
        for inner_at in range(row_at + 1, switches):
            running = running - factor[inner_at][row_at] * weights[inner_at]
        weights[row_at] = running / factor[row_at][row_at]
    return weights


def solve_kernel(
    fronts, inj, sw_from, sw_to, sw_susc, coupling, pivot, joined,
    yown, yrecv, zown, town, trecv, wown, wrecv, cown, crecv, xfull, xnext, injt,
    e_fwd, e_back, p_fwd, sw_wide, to_wide, susc_wide,
    inj_v, e_v, p_v,
    y_s, y_r, t_s, t_r, w_s, w_r, c_s, c_r, x_s, x_r, n_s, n_r, r_s, r_r, load,
):
    me, line = lax.axis_index("front"), lax.axis_index("line")
    other = 1 - line
    first, last = me == 0, me == fronts - 1
    bus, topo = inj.shape
    switches = sw_from.shape[0]
    rows = topo // (2 * CHUNKS)
    kinds = switches + 1
    pairs = [(i, c) for i in range(switches) for c in range(i + 2)]

    inj_load = pltpu.make_async_copy(inj, inj_v, load.at[0])
    e_load = pltpu.make_async_copy(coupling, e_v, load.at[1])
    p_load = pltpu.make_async_copy(pivot, p_v, load.at[2])
    inj_load.start()
    e_load.start()
    p_load.start()
    greet(me, other)

    @pl.when(jnp.logical_not(first))
    def _():
        greet(me - 1, line)

    @pl.when(jnp.logical_not(last))
    def _():
        greet(me + 1, line)

    def wide(ref, kind):
        fill = jnp.zeros((8 - switches, topo), kind)
        return jnp.concatenate([ref[...], fill], axis=0).T

    sw_wide[...] = wide(sw_from, jnp.int32)
    to_wide[...] = wide(sw_to, jnp.int32)
    susc_wide[...] = wide(sw_susc, F32)
    inj_load.wait()
    injt[...] = inj_v[...].T.reshape(injt.shape)

    def stack(c, carry):
        yown[c, 0:rows] = injt[line, c]
        ids = me * bus + lax.broadcasted_iota(jnp.int32, (rows, bus), 1)
        at = pl.ds(pl.multiple_of((line * CHUNKS + c) * rows, rows), rows)
        f, t = sw_wide[at, :], to_wide[at, :]

        def incidence(i, ids):
            return (ids == f[:, i:i + 1]).astype(F32) - (ids == t[:, i:i + 1]).astype(F32)

        for i in range(switches):
            part = slice((1 + i) * rows, (2 + i) * rows)
            yown[c, part] = incidence(i, ids)

            @pl.when(me == 1)
            def _():
                yrecv[c, part] = incidence(i, ids - bus)

        return carry

    lax.fori_loop(0, CHUNKS, stack, 0)
    pl.semaphore_wait(
        pltpu.get_barrier_semaphore(),
        1 + jnp.where(first, 0, 1) + jnp.where(last, 0, 1),
    )

    def y_copy(c):
        return copy_to(yown.at[c], yrecv.at[c], y_s.at[c], y_r.at[c], me + 1, line)

    def first_copy(c):
        part = pl.ds(0, rows)
        return copy_to(
            yown.at[c, part], yrecv.at[c, part], y_s.at[c], y_r.at[c], me + 1, line
        )

    def t_copy(c):
        return copy_to(town.at[c], trecv.at[c], t_s.at[c], t_r.at[c], me + 1, line)

    def w_copy(c):
        return copy_to(wown.at[c], wrecv.at[c], w_s.at[c], w_r.at[c], me - 1, line)

    def c_copy(c):
        return copy_to(cown.at[c], crecv.at[c], c_s.at[c], c_r.at[c], me - 1, line)

    def x_copy(c, half):
        place = xfull.at[half, c]
        return copy_to(place, place, x_s.at[c], x_r.at[c], me, other)

    def n_copy(c):
        return copy_to(
            xfull.at[line, c], xnext.at[line, c], n_s.at[c], n_r.at[c], me - 1, line
        )

    def r_copy(c, half):
        place = xnext.at[half, c]
        return copy_to(place, place, r_s.at[c], r_r.at[c], me, other)

    def relay(c):
        n_copy(c).wait_recv()
        r_copy(c, line).start()

    def each(fn):
        def step(c, carry):
            fn(c)
            return carry

        lax.fori_loop(0, CHUNKS, step, 0)

    @pl.when(first)
    def _():
        each(lambda c: first_copy(c).start())

    e_load.wait()
    e_fwd[0], e_fwd[1] = split(e_v[...].T)
    e_back[0], e_back[1] = split(e_v[...])
    p_load.wait()
    p_fwd[0], p_fwd[1] = split(p_v[...].T)
    lanes = lax.broadcasted_iota(jnp.int32, (rows, 128), 1)

    def back(c):
        w = wown[c]
        x = zown[c, 0:rows]
        for i in range(switches):
            x = x - zown[c, (1 + i) * rows:(2 + i) * rows] * w[:, i:i + 1]
        xfull[line, c] = x

        @pl.when(jnp.logical_not(last))
        def _():
            c_copy(c).wait_recv()
            xfull[line, c] = xfull[line, c] - crecv[c]

        @pl.when(jnp.logical_not(first))
        def _():
            cown[c] = product(xfull[line, c], e_back)
            c_copy(c).start()
            n_copy(c).start()

        x_copy(c, line).start()

    def ahead(c):
        @pl.when(jnp.logical_not(first))
        def _():
            @pl.when(me == 1)
            def _():
                first_copy(c).wait_recv()

            @pl.when(me > 1)
            def _():
                y_copy(c).wait_recv()

            yown[c] = yown[c] - product(yrecv[c], e_fwd)

            @pl.when(jnp.logical_not(last))
            def _():
                y_copy(c).start()

        y = yown[c]
        z = product(y, p_fwd)
        zown[c] = z
        block = jnp.zeros((rows, 128), F32)
        for j, (i, k) in enumerate(pairs):
            term = jnp.sum(
                y[(1 + i) * rows:(2 + i) * rows] * z[k * rows:(k + 1) * rows],
                axis=1, keepdims=True,
            )
            block = jnp.where(lanes == j, term, block)
        town[c] = block

        @pl.when(jnp.logical_not(first))
        def _():
            t_copy(c).wait_recv()
            town[c] = town[c] + trecv[c]

        @pl.when(jnp.logical_not(last))
        def _():
            t_copy(c).start()

        @pl.when(last)
        def _():
            total = town[c]
            terms = [[None] * kinds for i in range(switches)]
            for j, (i, k) in enumerate(pairs):
                terms[i][k] = total[:, j:j + 1]
            at = pl.ds(pl.multiple_of((line * CHUNKS + c) * rows, rows), rows)
            susc = susc_wide[at, :]
            weights = capacitance_solve(terms, [susc[:, i:i + 1] for i in range(switches)])
            w = jnp.zeros((rows, 128), F32)
            for i in range(switches):
                w = jnp.where(lanes == i, weights[i], w)
            wown[c] = w

            @pl.when(jnp.logical_not(first))
            def _():
                w_copy(c).start()

            back(c)

    each(ahead)

    @pl.when(jnp.logical_not(last))
    def _():
        def later(c):
            w_copy(c).wait_recv()
            wown[c] = wrecv[c]

            @pl.when(jnp.logical_not(first))
            def _():
                w_copy(c).start()

            back(c)

            @pl.when(c > 0)
            def _():
                relay(c - 1)

        each(later)
        relay(CHUNKS - 1)

    each(lambda c: x_copy(c, other).wait_recv())
    joined[0:bus] = xfull[...].reshape(topo, bus).T

    @pl.when(last)
    def _():
        joined[bus:2 * bus] = jnp.zeros((bus, topo), F32)

    @pl.when(jnp.logical_not(last))
    def _():
        each(lambda c: r_copy(c, other).wait_recv())
        joined[bus:2 * bus] = xnext[...].reshape(topo, bus).T

        def sent(c):
            @pl.when(first)
            def _():
                first_copy(c).wait_send()

            @pl.when(jnp.logical_not(first))
            def _():
                y_copy(c).wait_send()

            r_copy(c, line).wait_send()
            t_copy(c).wait_send()

        each(sent)

    @pl.when(jnp.logical_not(first))
    def _():
        def sent(c):
            w_copy(c).wait_send()
            c_copy(c).wait_send()
            n_copy(c).wait_send()

        each(sent)

    each(lambda c: x_copy(c, line).wait_send())


def pool_kernel(
    from_in, to_in, susc_in, owner_in, joined_in, weight, bias, acc, angles,
    br_from, br_to, br_susc, joined, flows, wide_w, wide_b, wide_t, load,
):
    hidden, topo = wide_w.shape
    bus = joined.shape[0] // 2
    first_bus = lax.axis_index("front") * bus
    pairs = [
        (from_in, br_from), (to_in, br_to), (susc_in, br_susc), (joined_in, joined),
    ]
    loads = [pltpu.make_async_copy(a, b, load.at[i]) for i, (a, b) in enumerate(pairs)]
    for one in loads:
        one.start()
    wide_w[...] = jnp.broadcast_to(weight[...], (topo, hidden)).T
    wide_b[...] = jnp.broadcast_to(bias[...], (topo, hidden)).T
    wide_t[...] = jnp.tanh(wide_b[...])
    owners, branches = acc.shape[0], flows.shape[0]
    names = lax.broadcasted_iota(jnp.int32, (owners, branches), 0)
    hot = (names == owner_in[...]).astype(F32).astype(BF16)
    for one in loads:
        one.wait()
    store = pltpu.make_async_copy(joined.at[pl.ds(0, bus)], angles, load.at[4])
    store.start()

    def bus_row(bus_id):
        at = jnp.minimum(jnp.maximum(bus_id - first_bus, 0), 2 * bus - 1)
        return joined[pl.ds(at, 1), :]

    def gather(g, carry):
        for u in range(UNROLL):
            at = g * UNROLL + u
            row = bus_row(br_from[at]) - bus_row(br_to[at])
            flows[pl.ds(at, 1), :] = br_susc[at] * row
        return carry

    lax.fori_loop(0, branches // UNROLL, gather, 0)

    def pool(g, carry):
        parts = []
        for u in range(WIDE):
            at = pl.ds(g * WIDE + u, 1)
            shifted = jnp.tanh(flows[...] * wide_w[at, :] + wide_b[at, :])
            parts.append((shifted - wide_t[at, :]).astype(BF16))
        for u in range(0, WIDE, 2):
            out = dot(hot, jnp.concatenate(parts[u:u + 2], axis=1))
            for v in range(2):
                for owner in range(owners):
                    acc[owner, pl.ds(g * WIDE + u + v, 1), :] = out[
                        owner:owner + 1, v * topo:(v + 1) * topo
                    ]
        return carry

    lax.fori_loop(0, hidden // WIDE, pool, 0)
    store.wait()


def share_kernel(fronts, acc, out_weight, scores, paired, summed, arrived, p_s, p_r, s_s, s_r):
    me, line = lax.axis_index("front"), lax.axis_index("line")
    other = 1 - line
    greet(me, other)

    def hello(step, carry):
        greet(lax.rem(me + step, fronts), line)
        return carry

    lax.fori_loop(1, fronts, hello, 0)
    pl.semaphore_wait(pltpu.get_barrier_semaphore(), fronts)

    def p_copy(f):
        return copy_to(acc.at[f * 2 + other], paired.at[f], p_s.at[f], p_r.at[f], me, other)

    def s_copy(f, origin, slot):
        return copy_to(summed.at[f], arrived.at[origin], s_s.at[f], s_r.at[slot], f, line)

    def turn(fn, own):
        def step(at, carry):
            fn(lax.rem(me + at, fronts))
            return carry

        lax.fori_loop(1, fronts + own, step, 0)

    turn(lambda f: p_copy(f).start(), 1)

    def pair(f):
        p_copy(f).wait_recv()
        summed[f] = acc[f * 2 + line] + paired[f]

        @pl.when(f != me)
        def _():
            s_copy(f, me, me).start()

    turn(pair, 1)
    turn(lambda f: s_copy(f, f, f).wait_recv(), 0)
    arrived[me] = summed[me]

    def add(f, total):
        return total + arrived[f]

    total = lax.fori_loop(1, fronts, add, arrived[0])
    pooled = (total * SCALE).T.astype(BF16)
    scores[...] = dot(pooled, out_weight[...]).astype(BF16)
    turn(lambda f: p_copy(f).wait_send(), 1)
    turn(lambda f: s_copy(f, me, me).wait_send(), 0)


def body(
    injections, switch_from, switch_to, switch_susc, coupling, pivot_inverse,
    branch_from, branch_to, branch_susc, branch_owner, in_weight, in_bias, out_weight,
):
    fronts = lax.axis_size("front")
    bus, topo = injections.shape
    switches = switch_from.shape[0]
    hidden = in_weight.shape[0]
    rows = topo // (2 * CHUNKS)
    many = (switches + 1) * rows
    owners = lax.axis_size(("front", "line"))
    vmem = pl.BlockSpec(memory_space=pltpu.VMEM)
    hbm = pl.BlockSpec(memory_space=pl.ANY)
    smem = pl.BlockSpec(memory_space=pltpu.SMEM)
    dma = pltpu.SemaphoreType.DMA
    full = lambda *shape: pltpu.VMEM(shape, F32)
    half = pltpu.VMEM((2, bus, bus), BF16)

    joined = pl.pallas_call(
        functools.partial(solve_kernel, fronts),
        out_shape=jax.ShapeDtypeStruct((2 * bus, topo), F32),
        in_specs=[hbm] + [vmem] * 3 + [hbm] * 2,
        out_specs=vmem,
        scratch_shapes=[
            full(CHUNKS, many, bus), full(CHUNKS, many, bus), full(CHUNKS, many, bus),
            full(CHUNKS, rows, 128), full(CHUNKS, rows, 128),
            full(CHUNKS, rows, 128), full(CHUNKS, rows, 128),
            full(CHUNKS, rows, bus), full(CHUNKS, rows, bus),
            full(2, CHUNKS, rows, bus), full(2, CHUNKS, rows, bus), full(2, CHUNKS, rows, bus),
            half, half, half,
            pltpu.VMEM((topo, 8), jnp.int32), pltpu.VMEM((topo, 8), jnp.int32), full(topo, 8),
            full(bus, topo), full(bus, bus), full(bus, bus),
        ] + [dma((CHUNKS,))] * 14 + [dma((3,))],
        compiler_params=pltpu.CompilerParams(
            collective_id=0, has_side_effects=True, vmem_limit_bytes=VMEM_BYTES
        ),
        name="solve",
    )(injections, switch_from, switch_to, switch_susc, coupling, pivot_inverse)

    branches = branch_from.shape[0]
    acc, angles = pl.pallas_call(
        pool_kernel,
        out_shape=(
            jax.ShapeDtypeStruct((owners, hidden, topo), F32),
            jax.ShapeDtypeStruct((bus, topo), F32),
        ),
        in_specs=[hbm] * 3 + [vmem] + [hbm] + [vmem] * 2,
        out_specs=(vmem, hbm),
        scratch_shapes=[
            pltpu.SMEM((branches,), jnp.int32), pltpu.SMEM((branches,), jnp.int32),
            pltpu.SMEM((branches,), F32), full(2 * bus, topo), full(branches, topo),
        ] + [full(hidden, topo)] * 3 + [dma((5,))],
        compiler_params=pltpu.CompilerParams(vmem_limit_bytes=VMEM_BYTES),
        name="pool",
    )(
        branch_from, branch_to, branch_susc, branch_owner.T, joined,
        in_weight[None], in_bias[None],
    )

    scores = pl.pallas_call(
        functools.partial(share_kernel, fronts),
        out_shape=jax.ShapeDtypeStruct((topo, out_weight.shape[1]), BF16),
        in_specs=[vmem] * 2,
        out_specs=vmem,
        scratch_shapes=[full(fronts, hidden, topo)] * 3 + [dma((fronts,))] * 4,
        compiler_params=pltpu.CompilerParams(
            collective_id=1, has_side_effects=True, vmem_limit_bytes=VMEM_BYTES
        ),
        name="share",
    )(acc, out_weight)
    return (scores[None], angles)


def solution(mesh):
    in_specs = (
        P("front", ("groups", "batch")),
        P(None, ("groups", "batch")),
        P(None, ("groups", "batch")),
        P(None, ("groups", "batch")),
        P("front", None),
        P("front", None),
        P(("front", "line")),
        P(("front", "line")),
        P(("front", "line")),
        P(("front", "line"), None),
        P(),
        P(),
        P(),
    )
    out_specs = (P(("front", "line"), ("groups", "batch"), None), P("front", ("groups", "batch")))
    return jax.shard_map(body, mesh=mesh, in_specs=in_specs, out_specs=out_specs, check_vma=False)
```

```python
import functools

import jax
import jax.numpy as jnp
from jax import lax
from jax.experimental import pallas as pl
from jax.experimental.pallas import tpu as pltpu
from jax.sharding import PartitionSpec as P

CHUNKS = 4
UNROLL = 8
WIDE = 16
PARTS = 4
SCALE = 512 ** (-0.5)
F32, BF16 = jnp.float32, jnp.bfloat16
VMEM_BYTES = 40 * 1024 * 1024


def split(value):
    high = value.astype(BF16)
    return high, (value - high.astype(F32)).astype(BF16)


def dot(operand, against):
    return jnp.dot(operand, against, preferred_element_type=F32)


def product(operand, against):
    high, low = split(operand)
    rows = operand.shape[0]
    both = dot(jnp.concatenate([high, low], axis=0), against[0])
    return both[:rows] + (both[rows:] + dot(high, against[1]))


def copy_to(src, dst, send_sem, recv_sem, front, line):
    return pltpu.make_async_remote_copy(
        src_ref=src,
        dst_ref=dst,
        send_sem=send_sem,
        recv_sem=recv_sem,
        device_id={"front": front, "line": line},
        device_id_type=pl.DeviceIdType.MESH,
    )


def greet(front, line):
    pl.semaphore_signal(
        pltpu.get_barrier_semaphore(),
        inc=1,
        device_id={"front": front, "line": line},
        device_id_type=pl.DeviceIdType.MESH,
    )


def capacitance_solve(terms, switch_susc):
    switches = len(switch_susc)
    factor = [[None] * switches for row_at in range(switches)]
    for row_at in range(switches):
        for col_at in range(row_at + 1):
            partial_sum = terms[row_at][1 + col_at]
            if row_at == col_at:
                partial_sum = partial_sum + 1.0 / switch_susc[row_at]
            for inner_at in range(col_at):
                partial_sum = partial_sum - factor[row_at][inner_at] * factor[col_at][inner_at]
            if row_at == col_at:
                factor[row_at][col_at] = jnp.sqrt(partial_sum)
            else:
                factor[row_at][col_at] = partial_sum / factor[col_at][col_at]
    lower_part = []
    for row_at in range(switches):
        running = terms[row_at][0]
        for inner_at in range(row_at):
            running = running - factor[row_at][inner_at] * lower_part[inner_at]
        lower_part.append(running / factor[row_at][row_at])
    weights = [None] * switches
    for row_at in reversed(range(switches)):
        running = lower_part[row_at]
        for inner_at in range(row_at + 1, switches):
            running = running - factor[inner_at][row_at] * weights[inner_at]
        weights[row_at] = running / factor[row_at][row_at]
    return weights


def solve_kernel(
    fronts, inj, sw_from, sw_to, sw_susc, coupling, pivot, joined,
    yown, yrecv, zown, town, trecv, wown, wrecv, cown, crecv, xfull, xnext, injt,
    e_fwd, e_back, p_fwd, sw_wide, to_wide, susc_wide,
    inj_v, e_v, p_v,
    y_s, y_r, t_s, t_r, w_s, w_r, c_s, c_r, x_s, x_r, n_s, n_r, r_s, r_r, load,
):
    me, line = lax.axis_index("front"), lax.axis_index("line")
    other = 1 - line
    first, last = me == 0, me == fronts - 1
    bus, topo = inj.shape
    switches = sw_from.shape[0]
    rows = topo // (2 * CHUNKS)
    kinds = switches + 1
    pairs = [(i, c) for i in range(switches) for c in range(i + 2)]

    inj_load = pltpu.make_async_copy(inj, inj_v, load.at[0])
    e_load = pltpu.make_async_copy(coupling, e_v, load.at[1])
    p_load = pltpu.make_async_copy(pivot, p_v, load.at[2])
    inj_load.start()
    e_load.start()
    p_load.start()
    greet(me, other)

    @pl.when(jnp.logical_not(first))
    def _():
        greet(me - 1, line)

    @pl.when(jnp.logical_not(last))
    def _():
        greet(me + 1, line)

    def wide(ref, kind):
        fill = jnp.zeros((8 - switches, topo), kind)
        return jnp.concatenate([ref[...], fill], axis=0).T

    sw_wide[...] = wide(sw_from, jnp.int32)
    to_wide[...] = wide(sw_to, jnp.int32)
    susc_wide[...] = wide(sw_susc, F32)
    inj_load.wait()
    injt[...] = inj_v[...].T.reshape(injt.shape)

    def stack(c, carry):
        yown[c, 0:rows] = injt[line, c]
        ids = me * bus + lax.broadcasted_iota(jnp.int32, (rows, bus), 1)
        at = pl.ds(pl.multiple_of((line * CHUNKS + c) * rows, rows), rows)
        f, t = sw_wide[at, :], to_wide[at, :]

        def incidence(i, ids):
            return (ids == f[:, i:i + 1]).astype(F32) - (ids == t[:, i:i + 1]).astype(F32)

        for i in range(switches):
            part = slice((1 + i) * rows, (2 + i) * rows)
            yown[c, part] = incidence(i, ids)

            @pl.when(me == 1)
            def _():
                yrecv[c, part] = incidence(i, ids - bus)

        return carry

    lax.fori_loop(0, CHUNKS, stack, 0)
    pl.semaphore_wait(
        pltpu.get_barrier_semaphore(),
        1 + jnp.where(first, 0, 1) + jnp.where(last, 0, 1),
    )

    def y_copy(c):
        return copy_to(yown.at[c], yrecv.at[c], y_s.at[c], y_r.at[c], me + 1, line)

    def first_copy(c):
        part = pl.ds(0, rows)
        return copy_to(
            yown.at[c, part], yrecv.at[c, part], y_s.at[c], y_r.at[c], me + 1, line
        )

    def t_copy(c):
        return copy_to(town.at[c], trecv.at[c], t_s.at[c], t_r.at[c], me + 1, line)

    def w_copy(c):
        return copy_to(wown.at[c], wrecv.at[c], w_s.at[c], w_r.at[c], me - 1, line)

    def c_copy(c):
        return copy_to(cown.at[c], crecv.at[c], c_s.at[c], c_r.at[c], me - 1, line)

    def x_copy(c, half):
        place = xfull.at[half, c]
        return copy_to(place, place, x_s.at[c], x_r.at[c], me, other)

    def n_copy(c):
        return copy_to(
            xfull.at[line, c], xnext.at[line, c], n_s.at[c], n_r.at[c], me - 1, line
        )

    def r_copy(c, half):
        place = xnext.at[half, c]
        return copy_to(place, place, r_s.at[c], r_r.at[c], me, other)

    def relay(c):
        n_copy(c).wait_recv()
        r_copy(c, line).start()

    def each(fn):
        def step(c, carry):
            fn(c)
            return carry

        lax.fori_loop(0, CHUNKS, step, 0)

    @pl.when(first)
    def _():
        each(lambda c: first_copy(c).start())

    e_load.wait()
    e_fwd[0], e_fwd[1] = split(e_v[...].T)
    e_back[0], e_back[1] = split(e_v[...])
    p_load.wait()
    p_fwd[0], p_fwd[1] = split(p_v[...].T)
    lanes = lax.broadcasted_iota(jnp.int32, (rows, 128), 1)

    def back(c):
        w = wown[c]
        x = zown[c, 0:rows]
        for i in range(switches):
            x = x - zown[c, (1 + i) * rows:(2 + i) * rows] * w[:, i:i + 1]
        xfull[line, c] = x

        @pl.when(jnp.logical_not(last))
        def _():
            c_copy(c).wait_recv()
            xfull[line, c] = xfull[line, c] - crecv[c]

        @pl.when(jnp.logical_not(first))
        def _():
            cown[c] = product(xfull[line, c], e_back)
            c_copy(c).start()
            n_copy(c).start()

        x_copy(c, line).start()

    def ahead(c):
        @pl.when(jnp.logical_not(first))
        def _():
            @pl.when(me == 1)
            def _():
                first_copy(c).wait_recv()

            @pl.when(me > 1)
            def _():
                y_copy(c).wait_recv()

            yown[c] = yown[c] - product(yrecv[c], e_fwd)

            @pl.when(jnp.logical_not(last))
            def _():
                y_copy(c).start()

        y = yown[c]
        z = product(y, p_fwd)
        zown[c] = z
        block = jnp.zeros((rows, 128), F32)
        for j, (i, k) in enumerate(pairs):
            term = jnp.sum(
                y[(1 + i) * rows:(2 + i) * rows] * z[k * rows:(k + 1) * rows],
                axis=1, keepdims=True,
            )
            block = jnp.where(lanes == j, term, block)
        town[c] = block

        @pl.when(jnp.logical_not(first))
        def _():
            t_copy(c).wait_recv()
            town[c] = town[c] + trecv[c]

        @pl.when(jnp.logical_not(last))
        def _():
            t_copy(c).start()

        @pl.when(last)
        def _():
            total = town[c]
            terms = [[None] * kinds for i in range(switches)]
            for j, (i, k) in enumerate(pairs):
                terms[i][k] = total[:, j:j + 1]
            at = pl.ds(pl.multiple_of((line * CHUNKS + c) * rows, rows), rows)
            susc = susc_wide[at, :]
            weights = capacitance_solve(terms, [susc[:, i:i + 1] for i in range(switches)])
            w = jnp.zeros((rows, 128), F32)
            for i in range(switches):
                w = jnp.where(lanes == i, weights[i], w)
            wown[c] = w

            @pl.when(jnp.logical_not(first))
            def _():
                w_copy(c).start()

            back(c)

    each(ahead)

    @pl.when(jnp.logical_not(last))
    def _():
        def later(c):
            w_copy(c).wait_recv()
            wown[c] = wrecv[c]

            @pl.when(jnp.logical_not(first))
            def _():
                w_copy(c).start()

            back(c)

            @pl.when(c > 0)
            def _():
                relay(c - 1)

        each(later)
        relay(CHUNKS - 1)

    each(lambda c: x_copy(c, other).wait_recv())
    joined[0:bus] = xfull[...].reshape(topo, bus).T

    @pl.when(last)
    def _():
        joined[bus:2 * bus] = jnp.zeros((bus, topo), F32)

    @pl.when(jnp.logical_not(last))
    def _():
        each(lambda c: r_copy(c, other).wait_recv())
        joined[bus:2 * bus] = xnext[...].reshape(topo, bus).T

        def sent(c):
            @pl.when(first)
            def _():
                first_copy(c).wait_send()

            @pl.when(jnp.logical_not(first))
            def _():
                y_copy(c).wait_send()

            r_copy(c, line).wait_send()
            t_copy(c).wait_send()

        each(sent)

    @pl.when(jnp.logical_not(first))
    def _():
        def sent(c):
            w_copy(c).wait_send()
            c_copy(c).wait_send()
            n_copy(c).wait_send()

        each(sent)

    each(lambda c: x_copy(c, line).wait_send())


def pool_kernel(
    fronts, from_in, to_in, susc_in, owner_in, joined_in, weight, bias, out_weight,
    scores, angles,
    br_from, br_to, br_susc, joined, flows, wide_w, wide_b, wide_t,
    acc, paired, summed, arrived, load, p_s, p_r, s_s, s_r,
):
    me, line = lax.axis_index("front"), lax.axis_index("line")
    other = 1 - line
    greet(me, other)

    def loop(start, stop, fn):
        def step(at, carry):
            fn(at)
            return carry

        lax.fori_loop(start, stop, step, 0)

    loop(1, fronts, lambda step: greet(lax.rem(me + step, fronts), line))
    hidden, topo = wide_w.shape
    bus = joined.shape[0] // 2
    first_bus = lax.axis_index("front") * bus
    pairs = [
        (from_in, br_from), (to_in, br_to), (susc_in, br_susc), (joined_in, joined),
    ]
    loads = [pltpu.make_async_copy(a, b, load.at[i]) for i, (a, b) in enumerate(pairs)]
    for one in loads:
        one.start()
    wide_w[...] = jnp.broadcast_to(weight[...], (topo, hidden)).T
    wide_b[...] = jnp.broadcast_to(bias[...], (topo, hidden)).T
    wide_t[...] = jnp.tanh(wide_b[...])
    owners, branches = acc.shape[0], flows.shape[0]
    names = lax.broadcasted_iota(jnp.int32, (owners, branches), 0)
    hot = (names == owner_in[...]).astype(F32).astype(BF16)
    for one in loads:
        one.wait()
    store = pltpu.make_async_copy(joined.at[pl.ds(0, bus)], angles, load.at[4])
    store.start()

    def bus_row(bus_id):
        at = jnp.minimum(jnp.maximum(bus_id - first_bus, 0), 2 * bus - 1)
        return joined[pl.ds(at, 1), :]

    def gather(g, carry):
        for u in range(UNROLL):
            at = g * UNROLL + u
            row = bus_row(br_from[at]) - bus_row(br_to[at])
            flows[pl.ds(at, 1), :] = br_susc[at] * row
        return carry

    lax.fori_loop(0, branches // UNROLL, gather, 0)

    def pool(g, carry):
        parts = []
        for u in range(WIDE):
            at = pl.ds(g * WIDE + u, 1)
            shifted = jnp.tanh(flows[...] * wide_w[at, :] + wide_b[at, :])
            parts.append((shifted - wide_t[at, :]).astype(BF16))
        for u in range(0, WIDE, 2):
            out = dot(hot, jnp.concatenate(parts[u:u + 2], axis=1))
            for v in range(2):
                for owner in range(owners):
                    acc[owner, pl.ds(g * WIDE + u + v, 1), :] = out[
                        owner:owner + 1, v * topo:(v + 1) * topo
                    ]
        return carry

    span = hidden // PARTS

    def part(q):
        return pl.ds(pl.multiple_of(q * span, span), span)

    def p_copy(q, f):
        return copy_to(
            acc.at[f * 2 + other, part(q)], paired.at[f, part(q)],
            p_s.at[q, f], p_r.at[q, f], me, other,
        )

    def s_copy(q, f, origin):
        return copy_to(
            summed.at[f, part(q)], arrived.at[origin, part(q)],
            s_s.at[q, f], s_r.at[q, origin], f, line,
        )

    def turned(at):
        return lax.rem(me + at, fronts)

    def work(q):
        lax.fori_loop(q * (span // WIDE), (q + 1) * (span // WIDE), pool, 0)

        @pl.when(q == 0)
        def _():
            pl.semaphore_wait(pltpu.get_barrier_semaphore(), fronts)

        loop(1, fronts + 1, lambda at: p_copy(q, turned(at)).start())

    def send_on(q):
        def one(at):
            f = turned(at)
            p_copy(q, f).wait_recv()
            summed[f, part(q)] = acc[f * 2 + line, part(q)] + paired[f, part(q)]

            @pl.when(f != me)
            def _():
                s_copy(q, f, me).start()

        loop(1, fronts + 1, one)

    def stage(q):
        work(q)

        @pl.when(q > 0)
        def _():
            send_on(q - 1)

    loop(0, PARTS, stage)
    send_on(PARTS - 1)
    arrived[me] = summed[me]

    def finish(q):
        def one(at):
            f = turned(at)
            s_copy(q, f, f).wait_recv()

        loop(1, fronts, one)

    loop(0, PARTS, finish)
    total = lax.fori_loop(1, fronts, lambda f, total: total + arrived[f], arrived[0])
    pooled = (total * SCALE).T.astype(BF16)
    scores[...] = dot(pooled, out_weight[...]).astype(BF16)

    def close(q):
        loop(1, fronts + 1, lambda at: p_copy(q, turned(at)).wait_send())
        loop(1, fronts, lambda at: s_copy(q, turned(at), me).wait_send())

    loop(0, PARTS, close)
    store.wait()


def body(
    injections, switch_from, switch_to, switch_susc, coupling, pivot_inverse,
    branch_from, branch_to, branch_susc, branch_owner, in_weight, in_bias, out_weight,
):
    fronts = lax.axis_size("front")
    bus, topo = injections.shape
    switches = switch_from.shape[0]
    hidden = in_weight.shape[0]
    rows = topo // (2 * CHUNKS)
    many = (switches + 1) * rows
    owners = lax.axis_size(("front", "line"))
    vmem = pl.BlockSpec(memory_space=pltpu.VMEM)
    hbm = pl.BlockSpec(memory_space=pltpu.HBM)
    smem = pl.BlockSpec(memory_space=pltpu.SMEM)
    dma = pltpu.SemaphoreType.DMA
    full = lambda *shape: pltpu.VMEM(shape, F32)
    half = pltpu.VMEM((2, bus, bus), BF16)

    joined = pl.pallas_call(
        functools.partial(solve_kernel, fronts),
        out_shape=jax.ShapeDtypeStruct((2 * bus, topo), F32),
        in_specs=[hbm] + [vmem] * 3 + [hbm] * 2,
        out_specs=vmem,
        scratch_shapes=[
            full(CHUNKS, many, bus), full(CHUNKS, many, bus), full(CHUNKS, many, bus),
            full(CHUNKS, rows, 128), full(CHUNKS, rows, 128),
            full(CHUNKS, rows, 128), full(CHUNKS, rows, 128),
            full(CHUNKS, rows, bus), full(CHUNKS, rows, bus),
            full(2, CHUNKS, rows, bus), full(2, CHUNKS, rows, bus), full(2, CHUNKS, rows, bus),
            half, half, half,
            pltpu.VMEM((topo, 8), jnp.int32), pltpu.VMEM((topo, 8), jnp.int32), full(topo, 8),
            full(bus, topo), full(bus, bus), full(bus, bus),
        ] + [dma((CHUNKS,))] * 14 + [dma((3,))],
        compiler_params=pltpu.CompilerParams(
            collective_id=0, has_side_effects=True, vmem_limit_bytes=VMEM_BYTES
        ),
        name="solve",
    )(injections, switch_from, switch_to, switch_susc, coupling, pivot_inverse)

    branches = branch_from.shape[0]
    scores, angles = pl.pallas_call(
        functools.partial(pool_kernel, fronts),
        out_shape=(
            jax.ShapeDtypeStruct((topo, out_weight.shape[1]), BF16),
            jax.ShapeDtypeStruct((bus, topo), F32),
        ),
        in_specs=[hbm] * 3 + [vmem] + [hbm] + [vmem] * 3,
        out_specs=(vmem, hbm),
        scratch_shapes=[
            pltpu.SMEM((branches,), jnp.int32), pltpu.SMEM((branches,), jnp.int32),
            pltpu.SMEM((branches,), F32), full(2 * bus, topo), full(branches, topo),
        ] + [full(hidden, topo)] * 3 + [full(owners, hidden, topo)]
        + [full(fronts, hidden, topo)] * 3 + [dma((5,))] + [dma((PARTS, fronts))] * 4,
        compiler_params=pltpu.CompilerParams(
            collective_id=1, has_side_effects=True, vmem_limit_bytes=VMEM_BYTES
        ),
        name="pool",
    )(
        branch_from, branch_to, branch_susc, branch_owner.T, joined,
        in_weight[None], in_bias[None], out_weight,
    )
    return (scores[None], angles)


def solution(mesh):
    in_specs = (
        P("front", ("groups", "batch")),
        P(None, ("groups", "batch")),
        P(None, ("groups", "batch")),
        P(None, ("groups", "batch")),
        P("front", None),
        P("front", None),
        P(("front", "line")),
        P(("front", "line")),
        P(("front", "line")),
        P(("front", "line"), None),
        P(),
        P(),
        P(),
    )
    out_specs = (P(("front", "line"), ("groups", "batch"), None), P("front", ("groups", "batch")))
    return jax.shard_map(body, mesh=mesh, in_specs=in_specs, out_specs=out_specs, check_vma=False)
```

```python
import functools

import jax
import jax.numpy as jnp
from jax import lax
from jax.experimental import pallas as pl
from jax.experimental.pallas import tpu as pltpu
from jax.sharding import PartitionSpec as P

CHUNKS = 4
UNROLL = 32
WIDE = 16
PARTS = 4
SCALE = 512 ** (-0.5)
F32, BF16 = jnp.float32, jnp.bfloat16
VMEM_BYTES = 40 * 1024 * 1024
SOLVE_BYTES = 60 * 1024 * 1024


def split(value):
    high = value.astype(BF16)
    return high, (value - high.astype(F32)).astype(BF16)


def dot(operand, against):
    return jnp.dot(operand, against, preferred_element_type=F32)


def product(operand, against):
    high, low = split(operand)
    rows = operand.shape[0]
    both = dot(jnp.concatenate([high, low], axis=0), against[0])
    return both[:rows] + (both[rows:] + dot(high, against[1]))


def copy_to(src, dst, send_sem, recv_sem, front, line):
    return pltpu.make_async_remote_copy(
        src_ref=src,
        dst_ref=dst,
        send_sem=send_sem,
        recv_sem=recv_sem,
        device_id={"front": front, "line": line},
        device_id_type=pl.DeviceIdType.MESH,
    )


def greet(front, line):
    pl.semaphore_signal(
        pltpu.get_barrier_semaphore(),
        inc=1,
        device_id={"front": front, "line": line},
        device_id_type=pl.DeviceIdType.MESH,
    )


def capacitance_solve(terms, switch_susc):
    switches = len(switch_susc)
    factor = [[None] * switches for row_at in range(switches)]
    for row_at in range(switches):
        for col_at in range(row_at + 1):
            partial_sum = terms[row_at][1 + col_at]
            if row_at == col_at:
                partial_sum = partial_sum + 1.0 / switch_susc[row_at]
            for inner_at in range(col_at):
                partial_sum = partial_sum - factor[row_at][inner_at] * factor[col_at][inner_at]
            if row_at == col_at:
                factor[row_at][col_at] = jnp.sqrt(partial_sum)
            else:
                factor[row_at][col_at] = partial_sum / factor[col_at][col_at]
    lower_part = []
    for row_at in range(switches):
        running = terms[row_at][0]
        for inner_at in range(row_at):
            running = running - factor[row_at][inner_at] * lower_part[inner_at]
        lower_part.append(running / factor[row_at][row_at])
    weights = [None] * switches
    for row_at in reversed(range(switches)):
        running = lower_part[row_at]
        for inner_at in range(row_at + 1, switches):
            running = running - factor[inner_at][row_at] * weights[inner_at]
        weights[row_at] = running / factor[row_at][row_at]
    return weights


def solve_kernel(
    fronts, inj, sw_from, sw_to, sw_susc, coupling, pivot, joined,
    yown, yrecv, zown, town, trecv, wown, wrecv, cown, crecv, xfull, xnext, injt,
    e_fwd, e_back, p_fwd, sw_wide, to_wide, susc_wide,
    inj_v, e_v, p_v,
    y_s, y_r, t_s, t_r, w_s, w_r, c_s, c_r, x_s, x_r, n_s, n_r, r_s, r_r, load,
):
    me, line = lax.axis_index("front"), lax.axis_index("line")
    other = 1 - line
    first, last = me == 0, me == fronts - 1
    bus, topo = inj.shape
    switches = sw_from.shape[0]
    rows = topo // (2 * CHUNKS)
    kinds = switches + 1
    pairs = [(i, c) for i in range(switches) for c in range(i + 2)]

    inj_load = pltpu.make_async_copy(inj, inj_v, load.at[0])
    e_load = pltpu.make_async_copy(coupling, e_v, load.at[1])
    p_load = pltpu.make_async_copy(pivot, p_v, load.at[2])
    inj_load.start()
    e_load.start()
    p_load.start()
    greet(me, other)

    @pl.when(jnp.logical_not(first))
    def _():
        greet(me - 1, line)

    @pl.when(jnp.logical_not(last))
    def _():
        greet(me + 1, line)

    def wide(ref, kind):
        fill = jnp.zeros((8 - switches, topo), kind)
        return jnp.concatenate([ref[...], fill], axis=0).T

    sw_wide[...] = wide(sw_from, jnp.int32)
    to_wide[...] = wide(sw_to, jnp.int32)
    susc_wide[...] = wide(sw_susc, F32)
    inj_load.wait()
    injt[...] = inj_v[...].T.reshape(injt.shape)

    def stack(c, carry):
        yown[c, 0:rows] = injt[line, c]
        ids = me * bus + lax.broadcasted_iota(jnp.int32, (rows, bus), 1)
        at = pl.ds(pl.multiple_of((line * CHUNKS + c) * rows, rows), rows)
        f, t = sw_wide[at, :], to_wide[at, :]

        def incidence(i, ids):
            return (ids == f[:, i:i + 1]).astype(F32) - (ids == t[:, i:i + 1]).astype(F32)

        for i in range(switches):
            part = slice((1 + i) * rows, (2 + i) * rows)
            yown[c, part] = incidence(i, ids)

            @pl.when(me == 1)
            def _():
                yrecv[c, part] = incidence(i, ids - bus)

        return carry

    lax.fori_loop(0, CHUNKS, stack, 0)
    pl.semaphore_wait(
        pltpu.get_barrier_semaphore(),
        1 + jnp.where(first, 0, 1) + jnp.where(last, 0, 1),
    )

    def y_copy(c):
        return copy_to(yown.at[c], yrecv.at[c], y_s.at[c], y_r.at[c], me + 1, line)

    def first_copy(c):
        part = pl.ds(0, rows)
        return copy_to(
            yown.at[c, part], yrecv.at[c, part], y_s.at[c], y_r.at[c], me + 1, line
        )

    def t_copy(c):
        return copy_to(town.at[c], trecv.at[c], t_s.at[c], t_r.at[c], me + 1, line)

    def w_copy(c):
        return copy_to(wown.at[c], wrecv.at[c], w_s.at[c], w_r.at[c], me - 1, line)

    def c_copy(c):
        return copy_to(cown.at[c], crecv.at[c], c_s.at[c], c_r.at[c], me - 1, line)

    def x_copy(c, half):
        place = xfull.at[half, c]
        return copy_to(place, place, x_s.at[c], x_r.at[c], me, other)

    def n_copy(c):
        return copy_to(
            xfull.at[line, c], xnext.at[line, c], n_s.at[c], n_r.at[c], me - 1, line
        )

    def r_copy(c, half):
        place = xnext.at[half, c]
        return copy_to(place, place, r_s.at[c], r_r.at[c], me, other)

    def relay(c):
        n_copy(c).wait_recv()
        r_copy(c, line).start()

    def each(fn):
        def step(c, carry):
            fn(c)
            return carry

        lax.fori_loop(0, CHUNKS, step, 0)

    @pl.when(first)
    def _():
        each(lambda c: first_copy(c).start())

    e_load.wait()
    e_fwd[0], e_fwd[1] = split(e_v[...].T)
    e_back[0], e_back[1] = split(e_v[...])
    p_load.wait()
    p_fwd[0], p_fwd[1] = split(p_v[...].T)
    lanes = lax.broadcasted_iota(jnp.int32, (rows, 128), 1)

    def back(c):
        w = wown[c]
        x = zown[c, 0:rows]
        for i in range(switches):
            x = x - zown[c, (1 + i) * rows:(2 + i) * rows] * w[:, i:i + 1]
        xfull[line, c] = x

        @pl.when(jnp.logical_not(last))
        def _():
            c_copy(c).wait_recv()
            xfull[line, c] = xfull[line, c] - crecv[c]

        @pl.when(jnp.logical_not(first))
        def _():
            cown[c] = product(xfull[line, c], e_back)
            c_copy(c).start()
            n_copy(c).start()

        x_copy(c, line).start()

    def ahead(c):
        @pl.when(jnp.logical_not(first))
        def _():
            @pl.when(me == 1)
            def _():
                first_copy(c).wait_recv()

            @pl.when(me > 1)
            def _():
                y_copy(c).wait_recv()

            yown[c] = yown[c] - product(yrecv[c], e_fwd)

            @pl.when(jnp.logical_not(last))
            def _():
                y_copy(c).start()

        y = yown[c]
        z = product(y, p_fwd)
        zown[c] = z
        block = jnp.zeros((rows, 128), F32)
        for j, (i, k) in enumerate(pairs):
            term = jnp.sum(
                y[(1 + i) * rows:(2 + i) * rows] * z[k * rows:(k + 1) * rows],
                axis=1, keepdims=True,
            )
            block = jnp.where(lanes == j, term, block)
        town[c] = block

        @pl.when(jnp.logical_not(first))
        def _():
            t_copy(c).wait_recv()
            town[c] = town[c] + trecv[c]

        @pl.when(jnp.logical_not(last))
        def _():
            t_copy(c).start()

        @pl.when(last)
        def _():
            total = town[c]
            terms = [[None] * kinds for i in range(switches)]
            for j, (i, k) in enumerate(pairs):
                terms[i][k] = total[:, j:j + 1]
            at = pl.ds(pl.multiple_of((line * CHUNKS + c) * rows, rows), rows)
            susc = susc_wide[at, :]
            weights = capacitance_solve(terms, [susc[:, i:i + 1] for i in range(switches)])
            w = jnp.zeros((rows, 128), F32)
            for i in range(switches):
                w = jnp.where(lanes == i, weights[i], w)
            wown[c] = w

            @pl.when(jnp.logical_not(first))
            def _():
                w_copy(c).start()

            back(c)

    each(ahead)

    @pl.when(jnp.logical_not(last))
    def _():
        def later(c):
            w_copy(c).wait_recv()
            wown[c] = wrecv[c]

            @pl.when(jnp.logical_not(first))
            def _():
                w_copy(c).start()

            back(c)

            @pl.when(c > 0)
            def _():
                relay(c - 1)

        each(later)
        relay(CHUNKS - 1)

    each(lambda c: x_copy(c, other).wait_recv())
    joined[0:bus] = xfull[...].reshape(topo, bus).T

    @pl.when(last)
    def _():
        joined[bus:2 * bus] = jnp.zeros((bus, topo), F32)

    @pl.when(jnp.logical_not(last))
    def _():
        each(lambda c: r_copy(c, other).wait_recv())
        joined[bus:2 * bus] = xnext[...].reshape(topo, bus).T

        def sent(c):
            @pl.when(first)
            def _():
                first_copy(c).wait_send()

            @pl.when(jnp.logical_not(first))
            def _():
                y_copy(c).wait_send()

            r_copy(c, line).wait_send()
            t_copy(c).wait_send()

        each(sent)

    @pl.when(jnp.logical_not(first))
    def _():
        def sent(c):
            w_copy(c).wait_send()
            c_copy(c).wait_send()
            n_copy(c).wait_send()

        each(sent)

    each(lambda c: x_copy(c, line).wait_send())


def pool_kernel(
    fronts, from_in, to_in, susc_in, owner_in, joined_in, weight, bias, out_weight,
    scores, angles,
    br_from, br_to, br_susc, joined, flows, wide_w, wide_b, wide_t,
    acc, paired, summed, arrived, load, p_s, p_r, s_s, s_r,
):
    me, line = lax.axis_index("front"), lax.axis_index("line")
    other = 1 - line
    greet(me, other)

    def loop(start, stop, fn):
        def step(at, carry):
            fn(at)
            return carry

        lax.fori_loop(start, stop, step, 0)

    loop(1, fronts, lambda step: greet(lax.rem(me + step, fronts), line))
    hidden, topo = wide_w.shape
    bus = joined.shape[0] // 2
    first_bus = lax.axis_index("front") * bus
    pairs = [
        (from_in, br_from), (to_in, br_to), (susc_in, br_susc), (joined_in, joined),
    ]
    loads = [pltpu.make_async_copy(a, b, load.at[i]) for i, (a, b) in enumerate(pairs)]
    for one in loads:
        one.start()
    wide_w[...] = jnp.broadcast_to(weight[...], (topo, hidden)).T
    wide_b[...] = jnp.broadcast_to(bias[...], (topo, hidden)).T
    wide_t[...] = jnp.tanh(wide_b[...])
    owners, branches = acc.shape[0], flows.shape[0]
    names = lax.broadcasted_iota(jnp.int32, (owners, branches), 0)
    hot = (names == owner_in[...]).astype(F32).astype(BF16)
    for one in loads:
        one.wait()
    store = pltpu.make_async_copy(joined.at[pl.ds(0, bus)], angles, load.at[4])
    store.start()

    def bus_row(bus_id):
        at = jnp.minimum(jnp.maximum(bus_id - first_bus, 0), 2 * bus - 1)
        return joined[pl.ds(at, 1), :]

    def gather(g, carry):
        for u in range(UNROLL):
            at = g * UNROLL + u
            row = bus_row(br_from[at]) - bus_row(br_to[at])
            flows[pl.ds(at, 1), :] = br_susc[at] * row
        return carry

    lax.fori_loop(0, branches // UNROLL, gather, 0)

    def pool(g, carry):
        parts = []
        for u in range(WIDE):
            at = pl.ds(g * WIDE + u, 1)
            shifted = jnp.tanh(flows[...] * wide_w[at, :] + wide_b[at, :])
            parts.append((shifted - wide_t[at, :]).astype(BF16))
        for u in range(0, WIDE, 2):
            out = dot(hot, jnp.concatenate(parts[u:u + 2], axis=1))
            for v in range(2):
                for owner in range(owners):
                    acc[owner, pl.ds(g * WIDE + u + v, 1), :] = out[
                        owner:owner + 1, v * topo:(v + 1) * topo
                    ]
        return carry

    span = hidden // PARTS

    def part(q):
        return pl.ds(pl.multiple_of(q * span, span), span)

    def p_copy(q, f):
        return copy_to(
            acc.at[f * 2 + other, part(q)], paired.at[f, part(q)],
            p_s.at[q, f], p_r.at[q, f], me, other,
        )

    def s_copy(q, f, origin):
        return copy_to(
            summed.at[f, part(q)], arrived.at[origin, part(q)],
            s_s.at[q, f], s_r.at[q, origin], f, line,
        )

    def turned(at):
        return lax.rem(me + at, fronts)

    def work(q):
        lax.fori_loop(q * (span // WIDE), (q + 1) * (span // WIDE), pool, 0)

        @pl.when(q == 0)
        def _():
            pl.semaphore_wait(pltpu.get_barrier_semaphore(), fronts)

        loop(1, fronts + 1, lambda at: p_copy(q, turned(at)).start())

    def send_on(q):
        def one(at):
            f = turned(at)
            p_copy(q, f).wait_recv()
            summed[f, part(q)] = acc[f * 2 + line, part(q)] + paired[f, part(q)]

            @pl.when(f != me)
            def _():
                s_copy(q, f, me).start()

        loop(1, fronts + 1, one)

    def stage(q):
        work(q)

        @pl.when(q > 0)
        def _():
            send_on(q - 1)

    loop(0, PARTS, stage)
    send_on(PARTS - 1)
    arrived[me] = summed[me]

    def finish(q):
        def one(at):
            f = turned(at)
            s_copy(q, f, f).wait_recv()

        loop(1, fronts, one)

    loop(0, PARTS, finish)
    total = lax.fori_loop(1, fronts, lambda f, total: total + arrived[f], arrived[0])
    pooled = (total * SCALE).T.astype(BF16)
    scores[...] = dot(pooled, out_weight[...]).astype(BF16)

    def close(q):
        loop(1, fronts + 1, lambda at: p_copy(q, turned(at)).wait_send())
        loop(1, fronts, lambda at: s_copy(q, turned(at), me).wait_send())

    loop(0, PARTS, close)
    store.wait()


def body(
    injections, switch_from, switch_to, switch_susc, coupling, pivot_inverse,
    branch_from, branch_to, branch_susc, branch_owner, in_weight, in_bias, out_weight,
):
    fronts = lax.axis_size("front")
    bus, topo = injections.shape
    switches = switch_from.shape[0]
    hidden = in_weight.shape[0]
    rows = topo // (2 * CHUNKS)
    many = (switches + 1) * rows
    owners = lax.axis_size(("front", "line"))
    vmem = pl.BlockSpec(memory_space=pltpu.VMEM)
    hbm = pl.BlockSpec(memory_space=pltpu.HBM)
    smem = pl.BlockSpec(memory_space=pltpu.SMEM)
    dma = pltpu.SemaphoreType.DMA
    full = lambda *shape: pltpu.VMEM(shape, F32)
    half = pltpu.VMEM((2, bus, bus), BF16)

    joined = pl.pallas_call(
        functools.partial(solve_kernel, fronts),
        out_shape=jax.ShapeDtypeStruct((2 * bus, topo), F32),
        in_specs=[hbm] + [vmem] * 3 + [hbm] * 2,
        out_specs=vmem,
        scratch_shapes=[
            full(CHUNKS, many, bus), full(CHUNKS, many, bus), full(CHUNKS, many, bus),
            full(CHUNKS, rows, 128), full(CHUNKS, rows, 128),
            full(CHUNKS, rows, 128), full(CHUNKS, rows, 128),
            full(CHUNKS, rows, bus), full(CHUNKS, rows, bus),
            full(2, CHUNKS, rows, bus), full(2, CHUNKS, rows, bus), full(2, CHUNKS, rows, bus),
            half, half, half,
            pltpu.VMEM((topo, 8), jnp.int32), pltpu.VMEM((topo, 8), jnp.int32), full(topo, 8),
            full(bus, topo), full(bus, bus), full(bus, bus),
        ] + [dma((CHUNKS,))] * 14 + [dma((3,))],
        compiler_params=pltpu.CompilerParams(
            collective_id=0, has_side_effects=True, vmem_limit_bytes=SOLVE_BYTES
        ),
        name="solve",
    )(injections, switch_from, switch_to, switch_susc, coupling, pivot_inverse)

    branches = branch_from.shape[0]
    scores, angles = pl.pallas_call(
        functools.partial(pool_kernel, fronts),
        out_shape=(
            jax.ShapeDtypeStruct((topo, out_weight.shape[1]), BF16),
            jax.ShapeDtypeStruct((bus, topo), F32),
        ),
        in_specs=[hbm] * 3 + [vmem] + [hbm] + [vmem] * 3,
        out_specs=(vmem, hbm),
        scratch_shapes=[
            pltpu.SMEM((branches,), jnp.int32), pltpu.SMEM((branches,), jnp.int32),
            pltpu.SMEM((branches,), F32), full(2 * bus, topo), full(branches, topo),
        ] + [full(hidden, topo)] * 3 + [full(owners, hidden, topo)]
        + [full(fronts, hidden, topo)] * 3 + [dma((5,))] + [dma((PARTS, fronts))] * 4,
        compiler_params=pltpu.CompilerParams(
            collective_id=1, has_side_effects=True, vmem_limit_bytes=VMEM_BYTES
        ),
        name="pool",
    )(
        branch_from, branch_to, branch_susc, branch_owner.T, joined,
        in_weight[None], in_bias[None], out_weight,
    )
    return (scores[None], angles)


def solution(mesh):
    in_specs = (
        P("front", ("groups", "batch")),
        P(None, ("groups", "batch")),
        P(None, ("groups", "batch")),
        P(None, ("groups", "batch")),
        P("front", None),
        P("front", None),
        P(("front", "line")),
        P(("front", "line")),
        P(("front", "line")),
        P(("front", "line"), None),
        P(),
        P(),
        P(),
    )
    out_specs = (P(("front", "line"), ("groups", "batch"), None), P("front", ("groups", "batch")))
    return jax.shard_map(body, mesh=mesh, in_specs=in_specs, out_specs=out_specs, check_vma=False)
```
